128 devices in a mesh: exp: 32 (over z, x, core), rep: 4 (over y).
Axes of the slice: x: 4, y: 4, z: 4, core: 2. Of those that a mesh axis runs over, the one named last changes fastest.
Arguments:
- images: bfloat16 [256, 256, 1024], P(('exp', 'rep')), may hold values from -12 to 12
- router: float32 [1024, 128], P(('exp', 'rep')), may hold values from -4 to 4
- w_in: bfloat16 [128, 1024, 2560], P(('exp', 'rep')), may hold values from -0.1875 to 0.1875
- w_out: bfloat16 [128, 2560, 1024], P(('exp', 'rep')), may hold values from -0.125 to 0.125
- out_grad: bfloat16 [256, 256, 1024], P(('exp', 'rep')), may hold values from -6 to 6
Outputs:
- images_grad: bfloat16 [256, 256, 1024], P(('exp', 'rep'))
- w_in_grad: bfloat16 [128, 1024, 2560], P(('exp', 'rep'))
- w_out_grad: bfloat16 [128, 2560, 1024], P(('exp', 'rep'))
- router_grad: float32 [1024, 128], P(('exp', 'rep'))
The draws below stay inside these ranges and needn't reach their ends.
All inputs are finite; a program needn't handle non-finite values.
Results may differ from the reference program's by a relative error of at most 0.012.
The reference program's roundings to bfloat16 on the way (of `router_low`, `slot_in`, `slot_grad`, `hidden`, `slot_out`, `pre_grad`, `slot_dx` and `logit_grad`) count: a program that leaves them out, or rounds other values in their place, can miss the bound.
Values may be sent and summed in bfloat16 or wider, within the bound.
No kernel may reach another device: no remote copies, remote signals or barrier semaphores. Data moves between devices by JAX's collectives and lax.ppermute only.
A program may use at most 128 MiB of HBM per device.

```python
import jax
import jax.numpy as jnp
from jax import lax

D = 1024
FF = 2560
TOK = 256
EXPERTS = 128
IMAGES = 256


def draw_router(key, part):
    key = jax.random.fold_in(key, 11)
    return jnp.clip(jax.random.normal(key, (D, EXPERTS), jnp.float32), -4.0, 4.0)


def draw_images(key, part):
    key = jax.random.fold_in(key, 23)
    sub_keys = jax.random.split(key, 2)
    scales = 0.5 * 6.0 ** jax.random.uniform(sub_keys[0], (IMAGES, TOK, 1), jnp.float32)
    return jnp.clip(scales * jax.random.normal(sub_keys[1], (IMAGES, TOK, D), jnp.float32), -12.0, 12.0).astype(jnp.bfloat16)


def levels(rng, dims, cuts, smallest, top_value):
    def one(position, shards_of):
        steps = jax.random.uniform(jax.random.fold_in(jax.random.fold_in(rng, 6), position), (shards_of,), jnp.float32, smallest / len(cuts), top_value / len(cuts))
        return jnp.repeat(jnp.exp(steps), dims[position] // shards_of).reshape((-1,) + (1,) * (len(dims) - position - 1))

    level = one(*cuts[0])
    for cut in cuts[1:]:
        level = level * one(*cut)
    return level


def noise(rng, dims, deviation, most, cuts=(), held_as=jnp.bfloat16):
    values = deviation * jax.random.normal(rng, dims, jnp.float32)
    if cuts:
        values = values * levels(rng, dims, cuts, -0.22, 0.18)
    return jnp.clip(values, -most, most).astype(held_as)


def setup_inputs(seed: int = 0) -> dict:
    arg_keys = jax.random.split(jax.random.key(seed), 6)
    return {
        "images": draw_images(jax.random.fold_in(arg_keys[5], 71), 0),
        "router": draw_router(jax.random.fold_in(arg_keys[5], 71), 0),
        "w_in": noise(arg_keys[2], (EXPERTS, D, FF), D ** -0.5, 0.1875, ((0, 128),)),
        "w_out": noise(arg_keys[3], (EXPERTS, FF, D), FF ** -0.5, 0.125, ((0, 128),)),
        "out_grad": noise(arg_keys[4], (IMAGES, TOK, D), 1.0, 6.0, ((0, 128),)),
    }


LOGIT_SCALE = 2.0
EPS = 1e-06
SQRT_HALF = 0.7071067811865476
INV_ROOT = 0.3989422804014327

def gelu_parts(pre_value):
    cumulative = 0.5 * (1.0 + lax.erf(pre_value * SQRT_HALF))
    gelu_slope = cumulative + pre_value * jnp.exp(-0.5 * pre_value * pre_value) * INV_ROOT
    return (pre_value * cumulative, gelu_slope)

def expert_pass(operands):
    slot_rows, slot_grads, weight_in, weight_out = operands
    pre_act = jnp.dot(slot_rows, weight_in, preferred_element_type=jnp.float32)
    activated, gelu_slope = gelu_parts(pre_act)
    hidden = activated.astype(jnp.bfloat16)
    slot_out = jnp.dot(hidden, weight_out, preferred_element_type=jnp.float32).astype(jnp.bfloat16)
    hidden_grad = jnp.dot(slot_grads, weight_out.T, preferred_element_type=jnp.float32)
    pre_grad = (hidden_grad * gelu_slope).astype(jnp.bfloat16)
    grad_out = jnp.dot(hidden.T, slot_grads, preferred_element_type=jnp.float32).astype(jnp.bfloat16)
    grad_in = jnp.dot(slot_rows.T, pre_grad, preferred_element_type=jnp.float32).astype(jnp.bfloat16)
    slot_dx = jnp.dot(pre_grad, weight_in.T, preferred_element_type=jnp.float32).astype(jnp.bfloat16)
    return (slot_out, slot_dx, grad_in, grad_out)

def reference(images, router, w_in, w_out, out_grad):
    inv_norm = lax.rsqrt(lax.optimization_barrier(jnp.sum(router * router, axis=0)) + EPS)
    router_hat = router * inv_norm
    router_low = router_hat.astype(jnp.bfloat16)
    low_wide = lax.optimization_barrier(router_low).astype(jnp.float32)
    images_wide = images.astype(jnp.float32)
    grad_wide = out_grad.astype(jnp.float32)
    logits = LOGIT_SCALE * jnp.einsum('btd,de->bte', images_wide, low_wide)
    dispatch = jax.nn.softmax(logits, axis=1)
    combine = jax.nn.softmax(logits, axis=2)
    dispatch_low = dispatch.astype(jnp.bfloat16)
    combine_low = combine.astype(jnp.bfloat16)
    slot_in = jnp.einsum('bte,btd->bed', dispatch_low.astype(jnp.float32), images_wide).astype(jnp.bfloat16)
    slot_grad = jnp.einsum('bte,btd->bed', combine_low.astype(jnp.float32), grad_wide).astype(jnp.bfloat16)
    results = lax.map(expert_pass, (jnp.transpose(slot_in, (1, 0, 2)), jnp.transpose(slot_grad, (1, 0, 2)), w_in, w_out))
    slot_out = jnp.transpose(results[0], (1, 0, 2)).astype(jnp.float32)
    slot_dx = jnp.transpose(results[1], (1, 0, 2)).astype(jnp.float32)
    combine_grad = jnp.einsum('btd,bed->bte', grad_wide, slot_out)
    grad_combine = combine * (combine_grad - lax.optimization_barrier(jnp.sum(combine * combine_grad, axis=2, keepdims=True)))
    dispatch_grad = jnp.einsum('btd,bed->bte', images_wide, slot_dx)
    grad_dispatch = dispatch * (dispatch_grad - lax.optimization_barrier(jnp.sum(dispatch * dispatch_grad, axis=1, keepdims=True)))
    logit_grad = (LOGIT_SCALE * (grad_combine + grad_dispatch)).astype(jnp.bfloat16)
    logit_wide = logit_grad.astype(jnp.float32)
    images_grad = (jnp.einsum('bte,bed->btd', dispatch_low.astype(jnp.float32), slot_dx) + jnp.einsum('bte,de->btd', logit_wide, low_wide)).astype(jnp.bfloat16)
    hat_grad = jnp.einsum('btd,bte->de', images_wide, logit_wide)
    moment = lax.optimization_barrier(jnp.sum(low_wide * hat_grad, axis=0))
    router_grad = (hat_grad - router_hat * moment) * inv_norm
    return (images_grad, results[2], results[3], router_grad)
```

```python
import jax
import jax.numpy as jnp
from jax import lax
from jax.sharding import PartitionSpec as P

LOGIT_SCALE = 2.0
EPS = 1e-06
AXES = ("exp", "rep")
SQRT_HALF = 0.7071067811865476
INV_ROOT = 0.3989422804014327


def gelu_parts(pre_value):
    cumulative = 0.5 * (1.0 + lax.erf(pre_value * SQRT_HALF))
    gelu_slope = cumulative + pre_value * jnp.exp(-0.5 * pre_value * pre_value) * INV_ROOT
    return (pre_value * cumulative, gelu_slope)


def contract_last(left_side, right_side):
    return lax.dot_general(
        left_side, right_side, (((1,), (1,)), ((), ())), preferred_element_type=jnp.float32
    )


def contract_first(left_side, right_side):
    return lax.dot_general(
        left_side, right_side, (((0,), (0,)), ((), ())), preferred_element_type=jnp.float32
    )


def expert_pass(slot_rows, slot_grads, weight_in, weight_out):
    pre_act = jnp.dot(slot_rows, weight_in, preferred_element_type=jnp.float32)
    activated, gelu_slope = gelu_parts(pre_act)
    hidden = activated.astype(jnp.bfloat16)
    slot_out = jnp.dot(hidden, weight_out, preferred_element_type=jnp.float32).astype(jnp.bfloat16)
    hidden_grad = contract_last(slot_grads, weight_out)
    pre_grad = (hidden_grad * gelu_slope).astype(jnp.bfloat16)
    grad_out = contract_first(hidden, slot_grads).astype(jnp.bfloat16)
    grad_in = contract_first(slot_rows, pre_grad).astype(jnp.bfloat16)
    slot_dx = contract_last(pre_grad, weight_in).astype(jnp.bfloat16)
    return (slot_out, slot_dx, grad_in, grad_out)


def spread_rows(rows):
    devices = lax.axis_size(AXES)
    copies = jnp.broadcast_to(rows[None], (devices,) + rows.shape)
    gathered = lax.all_to_all(copies, AXES, split_axis=0, concat_axis=0, tiled=True)
    return gathered.reshape(-1, rows.shape[1])


def per_device(images, router, w_in, w_out, out_grad):
    model_width = images.shape[2]
    router_whole = spread_rows(router)
    inv_norm = lax.rsqrt(jnp.sum(router_whole * router_whole, axis=0) + EPS)
    router_low = (router_whole * inv_norm).astype(jnp.bfloat16)
    logits = LOGIT_SCALE * jnp.einsum(
        "btd,de->bte", images, router_low, preferred_element_type=jnp.float32
    )
    dispatch = jax.nn.softmax(logits, axis=1)
    combine = jax.nn.softmax(logits, axis=2)
    dispatch_low = dispatch.astype(jnp.bfloat16)
    combine_low = combine.astype(jnp.bfloat16)
    slot_in = jnp.einsum(
        "bte,btd->bed", dispatch_low, images, preferred_element_type=jnp.float32
    ).astype(jnp.bfloat16)
    slot_grad = jnp.einsum(
        "bte,btd->bed", combine_low, out_grad, preferred_element_type=jnp.float32
    ).astype(jnp.bfloat16)
    paired = jnp.stack((slot_in, slot_grad), axis=0)
    arrived = lax.all_to_all(paired, ("exp", "rep"), split_axis=2, concat_axis=1, tiled=True)
    arrived = arrived.reshape(2, -1, model_width)
    slot_out, slot_dx, grad_in, grad_out = expert_pass(arrived[0], arrived[1], w_in[0], w_out[0])
    results = jnp.stack((slot_out, slot_dx), axis=0)
    returned = lax.all_to_all(
        results[:, :, None, :], ("exp", "rep"), split_axis=1, concat_axis=2, tiled=True
    )
    combine_grad = jnp.einsum(
        "btd,bed->bte", out_grad, returned[0], preferred_element_type=jnp.float32
    )
    grad_combine = combine * (combine_grad - jnp.sum(combine * combine_grad, axis=2, keepdims=True))
    dispatch_grad = jnp.einsum(
        "btd,bed->bte", images, returned[1], preferred_element_type=jnp.float32
    )
    grad_dispatch = dispatch * (
        dispatch_grad - jnp.sum(dispatch * dispatch_grad, axis=1, keepdims=True)
    )
    logit_grad = (LOGIT_SCALE * (grad_combine + grad_dispatch)).astype(jnp.bfloat16)
    images_grad = (
        jnp.einsum("bte,bed->btd", dispatch_low, returned[1], preferred_element_type=jnp.float32)
        + jnp.einsum("bte,de->btd", logit_grad, router_low, preferred_element_type=jnp.float32)
    ).astype(jnp.bfloat16)
    hat_part = jnp.einsum("btd,bte->de", images, logit_grad, preferred_element_type=jnp.float32)
    low_wide = lax.optimization_barrier(router_low).astype(jnp.float32)
    moment_part = jnp.sum(low_wide * hat_part, axis=0)
    devices = lax.axis_size(AXES)
    blocks = hat_part.reshape(devices, -1, hat_part.shape[1])
    own_rows = blocks.shape[1]
    moment_rows = jnp.broadcast_to(moment_part[None, None], (devices, 1, hat_part.shape[1]))
    sent = jnp.concatenate((blocks, moment_rows), axis=1)
    terms = lax.all_to_all(sent, AXES, split_axis=0, concat_axis=0, tiled=True)
    summed = jnp.sum(terms, axis=0)
    hat_rows, moment = summed[:own_rows], summed[own_rows]
    own_hat = router * inv_norm
    router_grad = (hat_rows - own_hat * moment) * inv_norm
    return (images_grad, grad_in[None], grad_out[None], router_grad)


def solution(mesh):
    in_specs = (
        P(("exp", "rep"), None, None),
        P(("exp", "rep"), None),
        P(("exp", "rep"), None, None),
        P(("exp", "rep"), None, None),
        P(("exp", "rep"), None, None),
    )
    out_specs = (
        P(("exp", "rep"), None, None),
        P(("exp", "rep"), None, None),
        P(("exp", "rep"), None, None),
        P(("exp", "rep"), None),
    )
    return jax.shard_map(
        per_device, mesh=mesh, in_specs=in_specs, out_specs=out_specs, check_vma=False
    )
```

```python
import jax
import jax.numpy as jnp
from jax import lax
from jax.experimental import pallas as pl
from jax.experimental.pallas import tpu as pltpu
from jax.sharding import PartitionSpec as P

LOGIT_SCALE = 2.0
EPS = 1e-06
SQRT_HALF = 0.7071067811865476
INV_ROOT = 0.3989422804014327
AXES = ("exp", "rep")
LANES = 128
FF_BLOCK = 512
VMEM_BYTES = 24 * 1024 * 1024


def gelu_parts(pre_value):
    cumulative = 0.5 * (1.0 + lax.erf(pre_value * SQRT_HALF))
    gelu_slope = cumulative + pre_value * jnp.exp(-0.5 * pre_value * pre_value) * INV_ROOT
    return (pre_value * cumulative, gelu_slope)


def contract_last(left_side, right_side):
    return lax.dot_general(
        left_side, right_side, (((1,), (1,)), ((), ())), preferred_element_type=jnp.float32
    )


def contract_first(left_side, right_side):
    return lax.dot_general(
        left_side, right_side, (((0,), (0,)), ((), ())), preferred_element_type=jnp.float32
    )


def exchange(blocks):
    return lax.all_to_all(blocks, AXES, split_axis=0, concat_axis=0, tiled=True)


def put_pair(messages_ref, pair, first, second):
    rows = first.shape[1] // LANES
    cut = [vectors.reshape(vectors.shape[0], rows, LANES) for vectors in (first, second)]
    messages_ref[:, 2 * pair * rows : 2 * (pair + 1) * rows, :] = jnp.concatenate(
        cut, axis=1
    ).astype(jnp.bfloat16)


def take_pair(messages_ref, pair, target_ref):
    peers, width = messages_ref.shape[0], target_ref.shape[1]
    rows = width // LANES
    turned = jnp.swapaxes(messages_ref[:, 2 * pair * rows : 2 * (pair + 1) * rows, :], 0, 1)
    for image in range(2):
        for chunk in range(rows):
            target_ref[
                image * peers : (image + 1) * peers, chunk * LANES : (chunk + 1) * LANES
            ] = turned[image * rows + chunk]


def pair_rows(ref, pair):
    rows = ref.shape[1] // 2
    return ref.at[:, pair * rows : (pair + 1) * rows, :]


def route_kernel(
    router_ref,
    images_ref,
    out_grad_hbm,
    sent_ref,
    low_ref,
    norm_ref,
    dispatch_ref,
    combine_ref,
    out_grad_ref,
    sem,
):
    fetch = pltpu.make_async_copy(out_grad_hbm, out_grad_ref, sem)
    fetch.start()
    whole = router_ref[...]
    inv_norm = lax.rsqrt(jnp.sum(whole * whole, axis=0, keepdims=True) + EPS)
    low = (whole * inv_norm).astype(jnp.bfloat16)
    low_ref[...] = low
    norm_ref[...] = inv_norm
    pictures = images_ref.shape[0]
    slot_in = []
    for image in range(pictures):
        tokens = images_ref[image]
        logits = LOGIT_SCALE * jnp.dot(tokens, low, preferred_element_type=jnp.float32)
        raised = jnp.exp(logits - jnp.max(logits, axis=0, keepdims=True))
        dispatch = raised / jnp.sum(raised, axis=0, keepdims=True)
        dispatch_ref[image] = dispatch
        slot_in.append(contract_first(dispatch.astype(jnp.bfloat16), tokens))
        raised = jnp.exp(logits - jnp.max(logits, axis=1, keepdims=True))
        combine_ref[image] = raised / jnp.sum(raised, axis=1, keepdims=True)
    put_pair(sent_ref, 0, *slot_in)
    fetch.wait()
    slot_grad = [
        contract_first(combine_ref[image].astype(jnp.bfloat16), out_grad_ref[image])
        for image in range(pictures)
    ]
    put_pair(sent_ref, 1, *slot_grad)


def expert_kernel(
    recv_ref,
    w_in_ref,
    w_out_ref,
    sent_hbm,
    rows_hbm,
    grads_hbm,
    hidden_hbm,
    pre_grad_hbm,
    sent_ref,
    rows_ref,
    grads_ref,
    hidden_ref,
    pre_grad_ref,
    slope_ref,
    sems,
):
    copies = []

    def write_out(source, target):
        copy = pltpu.make_async_copy(source, target, sems.at[len(copies)])
        copy.start()
        copies.append(copy)

    hidden_width = hidden_ref.shape[1]
    blocks = [slice(at, at + FF_BLOCK) for at in range(0, hidden_width, FF_BLOCK)]
    take_pair(recv_ref, 0, rows_ref)
    write_out(rows_ref, rows_hbm)
    take_pair(recv_ref, 1, grads_ref)
    write_out(grads_ref, grads_hbm)
    for block in blocks:
        activated, gelu_slope = gelu_parts(
            jnp.dot(rows_ref[...], w_in_ref[0, :, block], preferred_element_type=jnp.float32)
        )
        hidden_ref[:, block] = activated.astype(jnp.bfloat16)
        slope_ref[:, block] = gelu_slope
    write_out(hidden_ref, hidden_hbm)
    peers = recv_ref.shape[0]
    slot_out = jnp.dot(hidden_ref[...], w_out_ref[0], preferred_element_type=jnp.float32)
    put_pair(sent_ref, 0, slot_out[:peers], slot_out[peers:])
    write_out(pair_rows(sent_ref, 0), pair_rows(sent_hbm, 0))
    for block in blocks:
        hidden_grad = contract_last(grads_ref[...], w_out_ref[0, block, :])
        pre_grad_ref[:, block] = (hidden_grad * slope_ref[:, block]).astype(jnp.bfloat16)
    write_out(pre_grad_ref, pre_grad_hbm)
    slot_dx = contract_last(pre_grad_ref[...], w_in_ref[0])
    put_pair(sent_ref, 1, slot_dx[:peers], slot_dx[peers:])
    write_out(pair_rows(sent_ref, 1), pair_rows(sent_hbm, 1))
    for copy in copies:
        copy.wait()


def logit_kernel(
    recv_ref,
    router_ref,
    norm_ref,
    low_ref,
    images_ref,
    out_grad_ref,
    dispatch_ref,
    combine_ref,
    term_hbm,
    logit_grad_hbm,
    slot_dx_hbm,
    term_ref,
    logit_grad_ref,
    slot_dx_ref,
    slot_out_ref,
    sems,
):
    peers, width = recv_ref.shape[0], slot_out_ref.shape[1]
    take_pair(recv_ref, 1, slot_dx_ref)
    save_dx = pltpu.make_async_copy(slot_dx_ref, slot_dx_hbm, sems.at[0])
    save_dx.start()
    take_pair(recv_ref, 0, slot_out_ref)
    hat_turned = jnp.zeros((peers, width), jnp.float32)
    for image in range(images_ref.shape[0]):
        picked = slice(image * peers, (image + 1) * peers)
        combine, dispatch = combine_ref[image], dispatch_ref[image]
        combine_grad = contract_last(out_grad_ref[image], slot_out_ref[picked, :])
        grad_combine = combine * (
            combine_grad - jnp.sum(combine * combine_grad, axis=1, keepdims=True)
        )
        dispatch_grad = contract_last(images_ref[image], slot_dx_ref[picked, :])
        grad_dispatch = dispatch * (
            dispatch_grad - jnp.sum(dispatch * dispatch_grad, axis=0, keepdims=True)
        )
        logit_grad = (LOGIT_SCALE * (grad_combine + grad_dispatch)).astype(jnp.bfloat16)
        logit_grad_ref[image] = logit_grad
        hat_turned += contract_first(logit_grad, images_ref[image])
    save_logit = pltpu.make_async_copy(logit_grad_ref, logit_grad_hbm, sems.at[1])
    save_logit.start()
    hat_part = hat_turned.T
    moment_part = jnp.sum(low_ref[...].astype(jnp.float32) * hat_part, axis=0, keepdims=True)
    inv_norm = norm_ref[...]
    term_ref[...] = (hat_part - router_ref[...] * inv_norm * moment_part) * inv_norm
    save_term = pltpu.make_async_copy(term_ref, term_hbm, sems.at[2])
    save_term.start()
    save_dx.wait()
    save_logit.wait()
    save_term.wait()


def per_device(images, router, w_in, w_out, out_grad):
    pictures, tokens, width = images.shape
    own_rows, experts = router.shape
    devices = lax.axis_size(AXES)
    hidden_width = w_in.shape[2]
    rows = pictures * devices
    f32, bf16 = jnp.float32, jnp.bfloat16
    params = pltpu.CompilerParams(vmem_limit_bytes=VMEM_BYTES)
    in_vmem = pl.BlockSpec(memory_space=pltpu.VMEM)
    in_hbm = pl.BlockSpec(memory_space=pltpu.HBM)

    router_whole = exchange(jnp.broadcast_to(router[None], (devices, own_rows, experts)))
    router_whole = router_whole.reshape(width, experts)
    message = ((devices, 4 * width // LANES, LANES), bf16)
    per_token = ((pictures, tokens, experts), f32)
    sent, router_low, inv_norm, dispatch, combine = pl.pallas_call(
        route_kernel,
        in_specs=[in_vmem, in_vmem, in_hbm],
        out_specs=[in_vmem] * 5,
        out_shape=[
            jax.ShapeDtypeStruct(*message),
            jax.ShapeDtypeStruct((width, experts), bf16),
            jax.ShapeDtypeStruct((1, experts), f32),
            jax.ShapeDtypeStruct(*per_token),
            jax.ShapeDtypeStruct(*per_token),
        ],
        scratch_shapes=[pltpu.VMEM(out_grad.shape, bf16), pltpu.SemaphoreType.DMA],
        compiler_params=params,
        name="route",
    )(router_whole, images, pltpu.with_memory_space_constraint(out_grad, pltpu.HBM))

    arrived = exchange(sent)
    outs = [message] + [((rows, width), bf16)] * 2 + [((rows, hidden_width), bf16)] * 2
    sent, slot_rows, slot_grads, hidden, pre_grad = pl.pallas_call(
        expert_kernel,
        in_specs=[in_vmem] * 3,
        out_specs=[in_hbm] * 5,
        out_shape=[pltpu.HBM(*out) for out in outs],
        scratch_shapes=[pltpu.VMEM(*out) for out in outs]
        + [pltpu.VMEM((rows, hidden_width), f32), pltpu.SemaphoreType.DMA((6,))],
        compiler_params=params,
        name="expert",
    )(arrived, w_in, w_out)
    returned = exchange(sent)
    grad_out = contract_first(hidden, slot_grads).astype(bf16)
    grad_in = contract_first(slot_rows, pre_grad).astype(bf16)

    outs = [((width, experts), f32), ((pictures, tokens, experts), bf16), ((rows, width), bf16)]
    term, logit_grad, slot_dx = pl.pallas_call(
        logit_kernel,
        in_specs=[in_vmem] * 8,
        out_specs=[in_hbm] * 3,
        out_shape=[pltpu.HBM(*out) for out in outs],
        scratch_shapes=[pltpu.VMEM(*out) for out in outs]
        + [pltpu.VMEM((rows, width), bf16), pltpu.SemaphoreType.DMA((3,))],
        compiler_params=params,
        name="logit",
    )(returned, router_whole, inv_norm, router_low, images, out_grad, dispatch, combine)
    terms = exchange(term.reshape(devices, own_rows, experts))
    router_grad = jnp.sum(terms, axis=0)
    images_grad = (
        jnp.einsum(
            "bte,bed->btd",
            dispatch.astype(bf16),
            slot_dx.reshape(pictures, experts, width),
            preferred_element_type=f32,
        )
        + jnp.einsum("bte,de->btd", logit_grad, router_low, preferred_element_type=f32)
    ).astype(bf16)
    return (images_grad, grad_in[None], grad_out[None], router_grad)


def solution(mesh):
    in_specs = (
        P(AXES, None, None),
        P(AXES, None),
        P(AXES, None, None),
        P(AXES, None, None),
        P(AXES, None, None),
    )
    out_specs = (
        P(AXES, None, None),
        P(AXES, None, None),
        P(AXES, None, None),
        P(AXES, None),
    )
    return jax.shard_map(
        per_device, mesh=mesh, in_specs=in_specs, out_specs=out_specs, check_vma=False
    )
```

```python
import jax
import jax.numpy as jnp
from jax import lax
from jax.experimental import pallas as pl
from jax.experimental.pallas import tpu as pltpu
from jax.sharding import PartitionSpec as P

LOGIT_SCALE = 2.0
EPS = 1e-06
SQRT_HALF = 0.7071067811865476
INV_ROOT = 0.3989422804014327
AXES = ("exp", "rep")
LANES = 128
FF_BLOCK = 512
VMEM_BYTES = 24 * 1024 * 1024


def gelu_parts(pre_value):
    cumulative = 0.5 * (1.0 + lax.erf(pre_value * SQRT_HALF))
    gelu_slope = cumulative + pre_value * jnp.exp(-0.5 * pre_value * pre_value) * INV_ROOT
    return (pre_value * cumulative, gelu_slope)


def contract_last(left_side, right_side):
    return lax.dot_general(
        left_side, right_side, (((1,), (1,)), ((), ())), preferred_element_type=jnp.float32
    )


def contract_first(left_side, right_side):
    return lax.dot_general(
        left_side, right_side, (((0,), (0,)), ((), ())), preferred_element_type=jnp.float32
    )


def exchange(blocks):
    return lax.all_to_all(blocks, AXES, split_axis=0, concat_axis=0, tiled=True)


def put_pair(messages_ref, pair, first, second):
    rows = first.shape[1] // LANES
    cut = [vectors.reshape(vectors.shape[0], rows, LANES) for vectors in (first, second)]
    messages_ref[:, 2 * pair * rows : 2 * (pair + 1) * rows, :] = jnp.concatenate(
        cut, axis=1
    ).astype(jnp.bfloat16)


def take_pair(messages_ref, pair, target_ref):
    peers, width = messages_ref.shape[0], target_ref.shape[1]
    rows = width // LANES
    turned = jnp.swapaxes(messages_ref[:, 2 * pair * rows : 2 * (pair + 1) * rows, :], 0, 1)
    for image in range(2):
        for chunk in range(rows):
            target_ref[
                image * peers : (image + 1) * peers, chunk * LANES : (chunk + 1) * LANES
            ] = turned[image * rows + chunk]


def pair_rows(ref, pair):
    rows = ref.shape[1] // 2
    return ref.at[:, pair * rows : (pair + 1) * rows, :]


def spread_kernel(rows_ref, copies_ref):
    copies_ref[...] = jnp.broadcast_to(rows_ref[...][None], copies_ref.shape)


def route_kernel(
    router_ref,
    images_ref,
    out_grad_hbm,
    sent_ref,
    low_ref,
    norm_ref,
    dispatch_ref,
    combine_ref,
    out_grad_ref,
    sem,
):
    fetch = pltpu.make_async_copy(out_grad_hbm, out_grad_ref, sem)
    fetch.start()
    whole = router_ref[...]
    inv_norm = lax.rsqrt(jnp.sum(whole * whole, axis=0, keepdims=True) + EPS)
    low = (whole * inv_norm).astype(jnp.bfloat16)
    low_ref[...] = low
    norm_ref[...] = inv_norm
    pictures = images_ref.shape[0]
    slot_in = []
    for image in range(pictures):
        tokens = images_ref[image]
        logits = LOGIT_SCALE * jnp.dot(tokens, low, preferred_element_type=jnp.float32)
        raised = jnp.exp(logits - jnp.max(logits, axis=0, keepdims=True))
        dispatch = raised / jnp.sum(raised, axis=0, keepdims=True)
        dispatch_ref[image] = dispatch
        slot_in.append(contract_first(dispatch.astype(jnp.bfloat16), tokens))
        raised = jnp.exp(logits - jnp.max(logits, axis=1, keepdims=True))
        combine_ref[image] = raised / jnp.sum(raised, axis=1, keepdims=True)
    put_pair(sent_ref, 0, *slot_in)
    fetch.wait()
    slot_grad = [
        contract_first(combine_ref[image].astype(jnp.bfloat16), out_grad_ref[image])
        for image in range(pictures)
    ]
    put_pair(sent_ref, 1, *slot_grad)


def expert_kernel(
    recv_ref,
    w_in_ref,
    w_out_ref,
    sent_hbm,
    rows_hbm,
    grads_hbm,
    hidden_hbm,
    pre_grad_hbm,
    sent_ref,
    rows_ref,
    grads_ref,
    hidden_ref,
    pre_grad_ref,
    slope_ref,
    sems,
):
    copies = []

    def write_out(source, target):
        copy = pltpu.make_async_copy(source, target, sems.at[len(copies)])
        copy.start()
        copies.append(copy)

    hidden_width = hidden_ref.shape[1]
    blocks = [slice(at, at + FF_BLOCK) for at in range(0, hidden_width, FF_BLOCK)]
    take_pair(recv_ref, 0, rows_ref)
    write_out(rows_ref, rows_hbm)
    take_pair(recv_ref, 1, grads_ref)
    write_out(grads_ref, grads_hbm)
    for block in blocks:
        activated, gelu_slope = gelu_parts(
            jnp.dot(rows_ref[...], w_in_ref[0, :, block], preferred_element_type=jnp.float32)
        )
        hidden_ref[:, block] = activated.astype(jnp.bfloat16)
        slope_ref[:, block] = gelu_slope
    write_out(hidden_ref, hidden_hbm)
    peers = recv_ref.shape[0]
    slot_out = jnp.dot(hidden_ref[...], w_out_ref[0], preferred_element_type=jnp.float32)
    put_pair(sent_ref, 0, slot_out[:peers], slot_out[peers:])
    write_out(pair_rows(sent_ref, 0), pair_rows(sent_hbm, 0))
    for block in blocks:
        hidden_grad = contract_last(grads_ref[...], w_out_ref[0, block, :])
        pre_grad_ref[:, block] = (hidden_grad * slope_ref[:, block]).astype(jnp.bfloat16)
    write_out(pre_grad_ref, pre_grad_hbm)
    slot_dx = contract_last(pre_grad_ref[...], w_in_ref[0])
    put_pair(sent_ref, 1, slot_dx[:peers], slot_dx[peers:])
    write_out(pair_rows(sent_ref, 1), pair_rows(sent_hbm, 1))
    for copy in copies:
        copy.wait()


def logit_kernel(
    recv_hbm,
    router_ref,
    norm_ref,
    low_ref,
    images_ref,
    out_grad_ref,
    dispatch_ref,
    combine_ref,
    term_hbm,
    logit_grad_hbm,
    slot_dx_hbm,
    term_ref,
    logit_grad_ref,
    slot_dx_ref,
    slot_out_ref,
    recv_ref,
    sems,
):
    fetches = [
        pltpu.make_async_copy(pair_rows(recv_hbm, pair), pair_rows(recv_ref, pair), sems.at[3 + pair])
        for pair in range(2)
    ]
    fetches[1].start()
    fetches[0].start()
    peers, width = recv_ref.shape[0], slot_out_ref.shape[1]
    fetches[1].wait()
    take_pair(recv_ref, 1, slot_dx_ref)
    save_dx = pltpu.make_async_copy(slot_dx_ref, slot_dx_hbm, sems.at[0])
    save_dx.start()
    fetches[0].wait()
    take_pair(recv_ref, 0, slot_out_ref)
    hat_turned = jnp.zeros((peers, width), jnp.float32)
    for image in range(images_ref.shape[0]):
        picked = slice(image * peers, (image + 1) * peers)
        combine, dispatch = combine_ref[image], dispatch_ref[image]
        combine_grad = contract_last(out_grad_ref[image], slot_out_ref[picked, :])
        grad_combine = combine * (
            combine_grad - jnp.sum(combine * combine_grad, axis=1, keepdims=True)
        )
        dispatch_grad = contract_last(images_ref[image], slot_dx_ref[picked, :])
        grad_dispatch = dispatch * (
            dispatch_grad - jnp.sum(dispatch * dispatch_grad, axis=0, keepdims=True)
        )
        logit_grad = (LOGIT_SCALE * (grad_combine + grad_dispatch)).astype(jnp.bfloat16)
        logit_grad_ref[image] = logit_grad
        hat_turned += contract_first(logit_grad, images_ref[image])
    save_logit = pltpu.make_async_copy(logit_grad_ref, logit_grad_hbm, sems.at[1])
    save_logit.start()
    hat_part = hat_turned.T
    moment_part = jnp.sum(low_ref[...].astype(jnp.float32) * hat_part, axis=0, keepdims=True)
    inv_norm = norm_ref[...]
    term = (hat_part - router_ref[...] * inv_norm * moment_part) * inv_norm
    term_ref[...] = term.astype(jnp.bfloat16)
    save_term = pltpu.make_async_copy(term_ref, term_hbm, sems.at[2])
    save_term.start()
    save_dx.wait()
    save_logit.wait()
    save_term.wait()


def per_device(images, router, w_in, w_out, out_grad):
    pictures, tokens, width = images.shape
    own_rows, experts = router.shape
    devices = lax.axis_size(AXES)
    hidden_width = w_in.shape[2]
    rows = pictures * devices
    f32, bf16 = jnp.float32, jnp.bfloat16
    params = pltpu.CompilerParams(vmem_limit_bytes=VMEM_BYTES)
    in_vmem = pl.BlockSpec(memory_space=pltpu.VMEM)
    in_hbm = pl.BlockSpec(memory_space=pltpu.HBM)

    copies = pl.pallas_call(
        spread_kernel,
        in_specs=[in_vmem],
        out_specs=in_vmem,
        out_shape=jax.ShapeDtypeStruct((devices, own_rows, experts), f32),
        compiler_params=params,
        cost_estimate=pl.CostEstimate(
            flops=20_000_000_000, bytes_accessed=30_000_000, transcendentals=300_000
        ),
        name="spread",
    )(router)
    router_whole = exchange(copies).reshape(width, experts)
    message = ((devices, 4 * width // LANES, LANES), bf16)
    per_token = ((pictures, tokens, experts), f32)
    sent, router_low, inv_norm, dispatch, combine = pl.pallas_call(
        route_kernel,
        in_specs=[in_vmem, in_vmem, in_hbm],
        out_specs=[in_vmem] * 5,
        out_shape=[
            jax.ShapeDtypeStruct(*message),
            jax.ShapeDtypeStruct((width, experts), bf16),
            jax.ShapeDtypeStruct((1, experts), f32),
            jax.ShapeDtypeStruct(*per_token),
            jax.ShapeDtypeStruct(*per_token),
        ],
        scratch_shapes=[pltpu.VMEM(out_grad.shape, bf16), pltpu.SemaphoreType.DMA],
        compiler_params=params,
        name="route",
    )(router_whole, images, pltpu.with_memory_space_constraint(out_grad, pltpu.HBM))

    arrived = exchange(sent)
    outs = [message] + [((rows, width), bf16)] * 2 + [((rows, hidden_width), bf16)] * 2
    sent, slot_rows, slot_grads, hidden, pre_grad = pl.pallas_call(
        expert_kernel,
        in_specs=[in_vmem] * 3,
        out_specs=[in_hbm] * 5,
        out_shape=[pltpu.HBM(*out) for out in outs],
        scratch_shapes=[pltpu.VMEM(*out) for out in outs]
        + [
            pltpu.VMEM((rows, hidden_width), f32),
            pltpu.SemaphoreType.DMA((6,)),
        ],
        compiler_params=params,
        name="expert",
    )(arrived, w_in, w_out)
    returned = exchange(sent)
    grad_out = contract_first(hidden, slot_grads).astype(bf16)
    grad_in = contract_first(slot_rows, pre_grad).astype(bf16)

    outs = [((width, experts), bf16), ((pictures, tokens, experts), bf16), ((rows, width), bf16)]
    term, logit_grad, slot_dx = pl.pallas_call(
        logit_kernel,
        in_specs=[in_hbm] + [in_vmem] * 7,
        out_specs=[in_hbm] * 3,
        out_shape=[pltpu.HBM(*out) for out in outs],
        scratch_shapes=[pltpu.VMEM(*out) for out in outs]
        + [pltpu.VMEM((rows, width), bf16), pltpu.VMEM(*message), pltpu.SemaphoreType.DMA((5,))],
        compiler_params=params,
        name="logit",
    )(pltpu.with_memory_space_constraint(returned, pltpu.HBM), router_whole, inv_norm, router_low, images, out_grad, dispatch, combine)
    terms = exchange(term.reshape(devices, own_rows, experts))
    router_grad = jnp.sum(terms.astype(f32), axis=0)
    images_grad = (
        jnp.einsum(
            "bte,bed->btd",
            dispatch.astype(bf16),
            slot_dx.reshape(pictures, experts, width),
            preferred_element_type=f32,
        )
        + jnp.einsum("bte,de->btd", logit_grad, router_low, preferred_element_type=f32)
    ).astype(bf16)
    return (images_grad, grad_in[None], grad_out[None], router_grad)


def solution(mesh):
    in_specs = (
        P(AXES, None, None),
        P(AXES, None),
        P(AXES, None, None),
        P(AXES, None, None),
        P(AXES, None, None),
    )
    out_specs = (
        P(AXES, None, None),
        P(AXES, None, None),
        P(AXES, None, None),
        P(AXES, None),
    )
    return jax.shard_map(
        per_device, mesh=mesh, in_specs=in_specs, out_specs=out_specs, check_vma=False
    )
```

```python
import jax
import jax.numpy as jnp
from jax import lax
from jax.experimental import pallas as pl
from jax.experimental.pallas import tpu as pltpu
from jax.sharding import PartitionSpec as P

LOGIT_SCALE = 2.0
EPS = 1e-06
SQRT_HALF = 0.7071067811865476
INV_ROOT = 0.3989422804014327
AXES = ("exp", "rep")
LANES = 128
FF_BLOCK = 512
PAIR_CUTS = 4
VMEM_BYTES = 24 * 1024 * 1024


def gelu_parts(pre_value):
    cumulative = 0.5 * (1.0 + lax.erf(pre_value * SQRT_HALF))
    gelu_slope = cumulative + pre_value * jnp.exp(-0.5 * pre_value * pre_value) * INV_ROOT
    return (pre_value * cumulative, gelu_slope)


def contract_last(left_side, right_side):
    return lax.dot_general(
        left_side, right_side, (((1,), (1,)), ((), ())), preferred_element_type=jnp.float32
    )


def contract_first(left_side, right_side):
    return lax.dot_general(
        left_side, right_side, (((0,), (0,)), ((), ())), preferred_element_type=jnp.float32
    )


def exchange(blocks):
    return lax.all_to_all(blocks, AXES, split_axis=0, concat_axis=0, tiled=True)


def put_pair(messages_ref, pair, first, second):
    rows = first.shape[1] // LANES
    cut = [vectors.reshape(vectors.shape[0], rows, LANES) for vectors in (first, second)]
    messages_ref[:, 2 * pair * rows : 2 * (pair + 1) * rows, :] = jnp.concatenate(
        cut, axis=1
    ).astype(jnp.bfloat16)


def take_pair(messages_ref, pair, target_ref):
    peers, width = messages_ref.shape[0], target_ref.shape[1]
    rows = width // LANES
    turned = jnp.swapaxes(messages_ref[:, 2 * pair * rows : 2 * (pair + 1) * rows, :], 0, 1)
    for image in range(2):
        for chunk in range(rows):
            target_ref[
                image * peers : (image + 1) * peers, chunk * LANES : (chunk + 1) * LANES
            ] = turned[image * rows + chunk]


def pair_rows(ref, pair):
    rows = ref.shape[1] // 2
    return ref.at[:, pair * rows : (pair + 1) * rows, :]


def pair_copies(source, target, pair, sems, first_sem):
    peers = source.shape[0] // PAIR_CUTS
    return [
        pltpu.make_async_copy(
            pair_rows(source, pair).at[cut * peers : (cut + 1) * peers],
            pair_rows(target, pair).at[cut * peers : (cut + 1) * peers],
            sems.at[first_sem + cut],
        )
        for cut in range(PAIR_CUTS)
    ]


def spread_kernel(rows_ref, copies_ref):
    copies_ref[...] = jnp.broadcast_to(rows_ref[...][None], copies_ref.shape)


def route_kernel(
    router_ref,
    images_ref,
    out_grad_ref,
    sent_ref,
    low_ref,
    norm_ref,
    dispatch_ref,
    combine_ref,
):
    whole = router_ref[...]
    inv_norm = lax.rsqrt(jnp.sum(whole * whole, axis=0, keepdims=True) + EPS)
    low = (whole * inv_norm).astype(jnp.bfloat16)
    low_ref[...] = low
    norm_ref[...] = inv_norm
    pictures = images_ref.shape[0]
    slot_in = []
    for image in range(pictures):
        tokens = images_ref[image]
        logits = LOGIT_SCALE * jnp.dot(tokens, low, preferred_element_type=jnp.float32)
        raised = jnp.exp(logits - jnp.max(logits, axis=0, keepdims=True))
        dispatch = raised / jnp.sum(raised, axis=0, keepdims=True)
        dispatch_ref[image] = dispatch
        slot_in.append(contract_first(dispatch.astype(jnp.bfloat16), tokens))
        raised = jnp.exp(logits - jnp.max(logits, axis=1, keepdims=True))
        combine_ref[image] = raised / jnp.sum(raised, axis=1, keepdims=True)
    put_pair(sent_ref, 0, *slot_in)
    slot_grad = [
        contract_first(combine_ref[image].astype(jnp.bfloat16), out_grad_ref[image])
        for image in range(pictures)
    ]
    put_pair(sent_ref, 1, *slot_grad)


def expert_kernel(
    recv_ref,
    w_in_ref,
    w_out_ref,
    sent_hbm,
    rows_hbm,
    grads_hbm,
    hidden_hbm,
    pre_grad_hbm,
    sent_ref,
    rows_ref,
    grads_ref,
    hidden_ref,
    pre_grad_ref,
    slope_ref,
    sems,
):
    copies = []

    def write_out(source, target):
        copy = pltpu.make_async_copy(source, target, sems.at[len(copies)])
        copy.start()
        copies.append(copy)

    hidden_width = hidden_ref.shape[1]
    blocks = [slice(at, at + FF_BLOCK) for at in range(0, hidden_width, FF_BLOCK)]
    take_pair(recv_ref, 0, rows_ref)
    write_out(rows_ref, rows_hbm)
    take_pair(recv_ref, 1, grads_ref)
    write_out(grads_ref, grads_hbm)
    for block in blocks:
        activated, gelu_slope = gelu_parts(
            jnp.dot(rows_ref[...], w_in_ref[0, :, block], preferred_element_type=jnp.float32)
        )
        hidden_ref[:, block] = activated.astype(jnp.bfloat16)
        slope_ref[:, block] = gelu_slope
        write_out(hidden_ref.at[:, block], hidden_hbm.at[:, block])
    peers = recv_ref.shape[0]
    slot_out = jnp.dot(hidden_ref[...], w_out_ref[0], preferred_element_type=jnp.float32)
    put_pair(sent_ref, 0, slot_out[:peers], slot_out[peers:])
    for copy in pair_copies(sent_ref, sent_hbm, 0, sems, len(copies)):
        copy.start()
        copies.append(copy)
    for block in blocks:
        hidden_grad = contract_last(grads_ref[...], w_out_ref[0, block, :])
        pre_grad_ref[:, block] = (hidden_grad * slope_ref[:, block]).astype(jnp.bfloat16)
        write_out(pre_grad_ref.at[:, block], pre_grad_hbm.at[:, block])
    slot_dx = contract_last(pre_grad_ref[...], w_in_ref[0])
    put_pair(sent_ref, 1, slot_dx[:peers], slot_dx[peers:])
    for copy in pair_copies(sent_ref, sent_hbm, 1, sems, len(copies)):
        copy.start()
        copies.append(copy)
    for copy in copies:
        copy.wait()


def logit_kernel(
    recv_hbm,
    router_ref,
    norm_ref,
    low_ref,
    images_ref,
    out_grad_ref,
    dispatch_ref,
    combine_ref,
    term_hbm,
    logit_grad_hbm,
    slot_dx_hbm,
    term_ref,
    logit_grad_ref,
    slot_dx_ref,
    slot_out_ref,
    recv_ref,
    sems,
):
    fetches = [
        pair_copies(recv_hbm, recv_ref, pair, sems, 3 + pair * PAIR_CUTS) for pair in range(2)
    ]
    for copy in fetches[1] + fetches[0]:
        copy.start()
    peers, width = recv_ref.shape[0], slot_out_ref.shape[1]
    for copy in fetches[1]:
        copy.wait()
    take_pair(recv_ref, 1, slot_dx_ref)
    save_dx = pltpu.make_async_copy(slot_dx_ref, slot_dx_hbm, sems.at[0])
    save_dx.start()
    for copy in fetches[0]:
        copy.wait()
    take_pair(recv_ref, 0, slot_out_ref)
    logit_grads = []
    for image in range(images_ref.shape[0]):
        picked = slice(image * peers, (image + 1) * peers)
        combine, dispatch = combine_ref[image], dispatch_ref[image]
        combine_grad = contract_last(out_grad_ref[image], slot_out_ref[picked, :])
        grad_combine = combine * (
            combine_grad - jnp.sum(combine * combine_grad, axis=1, keepdims=True)
        )
        dispatch_grad = contract_last(images_ref[image], slot_dx_ref[picked, :])
        grad_dispatch = dispatch * (
            dispatch_grad - jnp.sum(dispatch * dispatch_grad, axis=0, keepdims=True)
        )
        logit_grad = (LOGIT_SCALE * (grad_combine + grad_dispatch)).astype(jnp.bfloat16)
        logit_grad_ref[image] = logit_grad
        logit_grads.append(logit_grad)
    save_logit = pltpu.make_async_copy(logit_grad_ref, logit_grad_hbm, sems.at[1])
    save_logit.start()
    all_tokens = images_ref[...].reshape(-1, width)
    hat_part = contract_first(jnp.concatenate(logit_grads, axis=0), all_tokens).T
    moment_part = jnp.sum(low_ref[...].astype(jnp.float32) * hat_part, axis=0, keepdims=True)
    inv_norm = norm_ref[...]
    term = (hat_part - router_ref[...] * inv_norm * moment_part) * inv_norm
    term_ref[...] = term.astype(jnp.bfloat16)
    save_term = pltpu.make_async_copy(term_ref, term_hbm, sems.at[2])
    save_term.start()
    save_dx.wait()
    save_logit.wait()
    save_term.wait()


def per_device(images, router, w_in, w_out, out_grad):
    pictures, tokens, width = images.shape
    own_rows, experts = router.shape
    devices = lax.axis_size(AXES)
    hidden_width = w_in.shape[2]
    rows = pictures * devices
    f32, bf16 = jnp.float32, jnp.bfloat16
    params = pltpu.CompilerParams(vmem_limit_bytes=VMEM_BYTES)
    in_vmem = pl.BlockSpec(memory_space=pltpu.VMEM)
    in_hbm = pl.BlockSpec(memory_space=pltpu.HBM)

    copies = pl.pallas_call(
        spread_kernel,
        in_specs=[in_vmem],
        out_specs=in_vmem,
        out_shape=jax.ShapeDtypeStruct((devices, own_rows, experts), f32),
        compiler_params=params,
        cost_estimate=pl.CostEstimate(
            flops=20_000_000_000, bytes_accessed=30_000_000, transcendentals=300_000
        ),
        name="spread",
    )(router)
    router_whole = exchange(copies).reshape(width, experts)
    message = ((devices, 4 * width // LANES, LANES), bf16)
    per_token = ((pictures, tokens, experts), f32)
    sent, router_low, inv_norm, dispatch, combine = pl.pallas_call(
        route_kernel,
        in_specs=[in_vmem] * 3,
        out_specs=[in_vmem] * 5,
        out_shape=[
            jax.ShapeDtypeStruct(*message),
            jax.ShapeDtypeStruct((width, experts), bf16),
            jax.ShapeDtypeStruct((1, experts), f32),
            jax.ShapeDtypeStruct(*per_token),
            jax.ShapeDtypeStruct(*per_token),
        ],
        compiler_params=params,
        name="route",
    )(router_whole, images, out_grad)

    arrived = exchange(sent)
    outs = [message] + [((rows, width), bf16)] * 2 + [((rows, hidden_width), bf16)] * 2
    sent, slot_rows, slot_grads, hidden, pre_grad = pl.pallas_call(
        expert_kernel,
        in_specs=[in_vmem] * 3,
        out_specs=[in_hbm] * 5,
        out_shape=[pltpu.HBM(*out) for out in outs],
        scratch_shapes=[pltpu.VMEM(*out) for out in outs]
        + [
            pltpu.VMEM((rows, hidden_width), f32),
            pltpu.SemaphoreType.DMA((2 + 2 * PAIR_CUTS + 2 * (hidden_width // FF_BLOCK),)),
        ],
        compiler_params=params,
        name="expert",
    )(arrived, w_in, w_out)
    returned = exchange(sent)
    grad_out = contract_first(hidden, slot_grads).astype(bf16)
    grad_in = contract_first(slot_rows, pre_grad).astype(bf16)

    outs = [((width, experts), bf16), ((pictures, tokens, experts), bf16), ((rows, width), bf16)]
    term, logit_grad, slot_dx = pl.pallas_call(
        logit_kernel,
        in_specs=[in_hbm] + [in_vmem] * 7,
        out_specs=[in_hbm] * 3,
        out_shape=[pltpu.HBM(*out) for out in outs],
        scratch_shapes=[pltpu.VMEM(*out) for out in outs]
        + [
            pltpu.VMEM((rows, width), bf16),
            pltpu.VMEM(*message),
            pltpu.SemaphoreType.DMA((3 + 2 * PAIR_CUTS,)),
        ],
        compiler_params=params,
        name="logit",
    )(pltpu.with_memory_space_constraint(returned, pltpu.HBM), router_whole, inv_norm, router_low, images, out_grad, dispatch, combine)
    terms = exchange(term.reshape(devices, own_rows, experts))
    router_grad = jnp.sum(terms.astype(f32), axis=0)
    images_grad = (
        jnp.einsum(
            "bte,bed->btd",
            dispatch.astype(bf16),
            slot_dx.reshape(pictures, experts, width),
            preferred_element_type=f32,
        )
        + jnp.einsum("bte,de->btd", logit_grad, router_low, preferred_element_type=f32)
    ).astype(bf16)
    return (images_grad, grad_in[None], grad_out[None], router_grad)


def solution(mesh):
    in_specs = (
        P(AXES, None, None),
        P(AXES, None),
        P(AXES, None, None),
        P(AXES, None, None),
        P(AXES, None, None),
    )
    out_specs = (
        P(AXES, None, None),
        P(AXES, None, None),
        P(AXES, None, None),
        P(AXES, None),
    )
    return jax.shard_map(
        per_device, mesh=mesh, in_specs=in_specs, out_specs=out_specs, check_vma=False
    )
```

```python
import jax
import jax.numpy as jnp
from jax import lax
from jax.experimental import pallas as pl
from jax.experimental.pallas import tpu as pltpu
from jax.sharding import PartitionSpec as P

LOGIT_SCALE = 2.0
EPS = 1e-06
SQRT_HALF = 0.7071067811865476
INV_ROOT = 0.3989422804014327
AXES = ("exp", "rep")
LANES = 128
FF_BLOCK = 1280
PAIR_CUTS = 4
VMEM_BYTES = 24 * 1024 * 1024


def gelu_parts(pre_value):
    cumulative = 0.5 * (1.0 + lax.erf(pre_value * SQRT_HALF))
    gelu_slope = cumulative + pre_value * jnp.exp(-0.5 * pre_value * pre_value) * INV_ROOT
    return (pre_value * cumulative, gelu_slope)


def contract_last(left_side, right_side):
    return lax.dot_general(
        left_side, right_side, (((1,), (1,)), ((), ())), preferred_element_type=jnp.float32
    )


def contract_first(left_side, right_side):
    return lax.dot_general(
        left_side, right_side, (((0,), (0,)), ((), ())), preferred_element_type=jnp.float32
    )


def exchange(blocks):
    return lax.all_to_all(blocks, AXES, split_axis=0, concat_axis=0, tiled=True)


def put_pair(messages_ref, pair, first, second):
    rows = first.shape[1] // LANES
    cut = [vectors.reshape(vectors.shape[0], rows, LANES) for vectors in (first, second)]
    messages_ref[:, 2 * pair * rows : 2 * (pair + 1) * rows, :] = jnp.concatenate(
        cut, axis=1
    ).astype(jnp.bfloat16)


def take_pair(messages_ref, pair, target_ref):
    peers, width = messages_ref.shape[0], target_ref.shape[1]
    rows = width // LANES
    turned = jnp.swapaxes(messages_ref[:, 2 * pair * rows : 2 * (pair + 1) * rows, :], 0, 1)
    for image in range(2):
        for chunk in range(rows):
            target_ref[
                image * peers : (image + 1) * peers, chunk * LANES : (chunk + 1) * LANES
            ] = turned[image * rows + chunk]


def pair_rows(ref, pair):
    rows = ref.shape[1] // 2
    return ref.at[:, pair * rows : (pair + 1) * rows, :]


def pair_copies(source, target, pair, sems, first_sem):
    peers = source.shape[0] // PAIR_CUTS
    return [
        pltpu.make_async_copy(
            pair_rows(source, pair).at[cut * peers : (cut + 1) * peers],
            pair_rows(target, pair).at[cut * peers : (cut + 1) * peers],
            sems.at[first_sem + cut],
        )
        for cut in range(PAIR_CUTS)
    ]


def spread_kernel(rows_ref, copies_ref):
    copies_ref[...] = jnp.broadcast_to(rows_ref[...][None], copies_ref.shape)


def route_kernel(
    router_ref,
    images_ref,
    out_grad_ref,
    sent_ref,
    low_ref,
    norm_ref,
    dispatch_ref,
    combine_ref,
):
    whole = router_ref[...]
    inv_norm = lax.rsqrt(jnp.sum(whole * whole, axis=0, keepdims=True) + EPS)
    low = (whole * inv_norm).astype(jnp.bfloat16)
    low_ref[...] = low
    norm_ref[...] = inv_norm
    pictures = images_ref.shape[0]
    slot_in = []
    for image in range(pictures):
        tokens = images_ref[image]
        logits = LOGIT_SCALE * jnp.dot(tokens, low, preferred_element_type=jnp.float32)
        raised = jnp.exp(logits - jnp.max(logits, axis=0, keepdims=True))
        dispatch = raised / jnp.sum(raised, axis=0, keepdims=True)
        dispatch_ref[image] = dispatch
        slot_in.append(contract_first(dispatch.astype(jnp.bfloat16), tokens))
        raised = jnp.exp(logits - jnp.max(logits, axis=1, keepdims=True))
        combine_ref[image] = raised / jnp.sum(raised, axis=1, keepdims=True)
    put_pair(sent_ref, 0, *slot_in)
    slot_grad = [
        contract_first(combine_ref[image].astype(jnp.bfloat16), out_grad_ref[image])
        for image in range(pictures)
    ]
    put_pair(sent_ref, 1, *slot_grad)


def expert_kernel(
    recv_ref,
    w_in_ref,
    w_out_ref,
    sent_hbm,
    rows_hbm,
    grads_hbm,
    hidden_hbm,
    pre_grad_hbm,
    sent_ref,
    rows_ref,
    grads_ref,
    hidden_ref,
    pre_grad_ref,
    slope_ref,
    sems,
):
    copies = []

    def write_out(source, target):
        copy = pltpu.make_async_copy(source, target, sems.at[len(copies)])
        copy.start()
        copies.append(copy)

    hidden_width = hidden_ref.shape[1]
    blocks = [slice(at, at + FF_BLOCK) for at in range(0, hidden_width, FF_BLOCK)]
    take_pair(recv_ref, 0, rows_ref)
    write_out(rows_ref, rows_hbm)
    take_pair(recv_ref, 1, grads_ref)
    write_out(grads_ref, grads_hbm)
    for block in blocks:
        activated, gelu_slope = gelu_parts(
            jnp.dot(rows_ref[...], w_in_ref[0, :, block], preferred_element_type=jnp.float32)
        )
        hidden_ref[:, block] = activated.astype(jnp.bfloat16)
        slope_ref[:, block] = gelu_slope
        write_out(hidden_ref.at[:, block], hidden_hbm.at[:, block])
    peers = recv_ref.shape[0]
    slot_out = jnp.dot(hidden_ref[...], w_out_ref[0], preferred_element_type=jnp.float32)
    put_pair(sent_ref, 0, slot_out[:peers], slot_out[peers:])
    for copy in pair_copies(sent_ref, sent_hbm, 0, sems, len(copies)):
        copy.start()
        copies.append(copy)
    for block in blocks:
        hidden_grad = contract_last(grads_ref[...], w_out_ref[0, block, :])
        pre_grad_ref[:, block] = (hidden_grad * slope_ref[:, block]).astype(jnp.bfloat16)
        write_out(pre_grad_ref.at[:, block], pre_grad_hbm.at[:, block])
    slot_dx = contract_last(pre_grad_ref[...], w_in_ref[0])
    put_pair(sent_ref, 1, slot_dx[:peers], slot_dx[peers:])
    for copy in pair_copies(sent_ref, sent_hbm, 1, sems, len(copies)):
        copy.start()
        copies.append(copy)
    for copy in copies:
        copy.wait()


def logit_kernel(
    recv_hbm,
    router_ref,
    norm_ref,
    low_ref,
    images_ref,
    out_grad_ref,
    dispatch_ref,
    combine_ref,
    term_hbm,
    logit_grad_hbm,
    slot_dx_hbm,
    term_ref,
    logit_grad_ref,
    slot_dx_ref,
    slot_out_ref,
    recv_ref,
    sems,
):
    fetches = [
        pair_copies(recv_hbm, recv_ref, pair, sems, 3 + pair * PAIR_CUTS) for pair in range(2)
    ]
    for copy in fetches[1] + fetches[0]:
        copy.start()
    peers, width = recv_ref.shape[0], slot_out_ref.shape[1]
    for copy in fetches[1]:
        copy.wait()
    take_pair(recv_ref, 1, slot_dx_ref)
    save_dx = pltpu.make_async_copy(slot_dx_ref, slot_dx_hbm, sems.at[0])
    save_dx.start()
    for copy in fetches[0]:
        copy.wait()
    take_pair(recv_ref, 0, slot_out_ref)
    logit_grads = []
    for image in range(images_ref.shape[0]):
        picked = slice(image * peers, (image + 1) * peers)
        combine, dispatch = combine_ref[image], dispatch_ref[image]
        combine_grad = contract_last(out_grad_ref[image], slot_out_ref[picked, :])
        grad_combine = combine * (
            combine_grad - jnp.sum(combine * combine_grad, axis=1, keepdims=True)
        )
        dispatch_grad = contract_last(images_ref[image], slot_dx_ref[picked, :])
        grad_dispatch = dispatch * (
            dispatch_grad - jnp.sum(dispatch * dispatch_grad, axis=0, keepdims=True)
        )
        logit_grad = (LOGIT_SCALE * (grad_combine + grad_dispatch)).astype(jnp.bfloat16)
        logit_grad_ref[image] = logit_grad
        logit_grads.append(logit_grad)
    save_logit = pltpu.make_async_copy(logit_grad_ref, logit_grad_hbm, sems.at[1])
    save_logit.start()
    all_tokens = images_ref[...].reshape(-1, width)
    hat_part = contract_first(jnp.concatenate(logit_grads, axis=0), all_tokens).T
    moment_part = jnp.sum(low_ref[...].astype(jnp.float32) * hat_part, axis=0, keepdims=True)
    inv_norm = norm_ref[...]
    term = (hat_part - router_ref[...] * inv_norm * moment_part) * inv_norm
    term_ref[...] = term.astype(jnp.bfloat16)
    save_term = pltpu.make_async_copy(term_ref, term_hbm, sems.at[2])
    save_term.start()
    save_dx.wait()
    save_logit.wait()
    save_term.wait()


def per_device(images, router, w_in, w_out, out_grad):
    pictures, tokens, width = images.shape
    own_rows, experts = router.shape
    devices = lax.axis_size(AXES)
    hidden_width = w_in.shape[2]
    rows = pictures * devices
    f32, bf16 = jnp.float32, jnp.bfloat16
    params = pltpu.CompilerParams(vmem_limit_bytes=VMEM_BYTES)
    in_vmem = pl.BlockSpec(memory_space=pltpu.VMEM)
    in_hbm = pl.BlockSpec(memory_space=pltpu.HBM)

    copies = pl.pallas_call(
        spread_kernel,
        in_specs=[in_vmem],
        out_specs=in_vmem,
        out_shape=jax.ShapeDtypeStruct((devices, own_rows, experts), f32),
        compiler_params=params,
        cost_estimate=pl.CostEstimate(
            flops=20_000_000_000, bytes_accessed=30_000_000, transcendentals=300_000
        ),
        name="spread",
    )(router)
    router_whole = exchange(copies).reshape(width, experts)
    message = ((devices, 4 * width // LANES, LANES), bf16)
    per_token = ((pictures, tokens, experts), f32)
    sent, router_low, inv_norm, dispatch, combine = pl.pallas_call(
        route_kernel,
        in_specs=[in_vmem] * 3,
        out_specs=[in_vmem] * 5,
        out_shape=[
            jax.ShapeDtypeStruct(*message),
            jax.ShapeDtypeStruct((width, experts), bf16),
            jax.ShapeDtypeStruct((1, experts), f32),
            jax.ShapeDtypeStruct(*per_token),
            jax.ShapeDtypeStruct(*per_token),
        ],
        compiler_params=params,
        name="route",
    )(router_whole, images, out_grad)

    arrived = exchange(sent)
    outs = [message] + [((rows, width), bf16)] * 2 + [((rows, hidden_width), bf16)] * 2
    sent, slot_rows, slot_grads, hidden, pre_grad = pl.pallas_call(
        expert_kernel,
        in_specs=[in_vmem] * 3,
        out_specs=[in_hbm] * 5,
        out_shape=[pltpu.HBM(*out) for out in outs],
        scratch_shapes=[pltpu.VMEM(*out) for out in outs]
        + [
            pltpu.VMEM((rows, hidden_width), f32),
            pltpu.SemaphoreType.DMA((2 + 2 * PAIR_CUTS + 2 * (hidden_width // FF_BLOCK),)),
        ],
        compiler_params=params,
        name="expert",
    )(arrived, w_in, w_out)
    returned = exchange(sent)
    grad_out = contract_first(hidden, slot_grads).astype(bf16)
    grad_in = contract_first(slot_rows, pre_grad).astype(bf16)

    outs = [((width, experts), bf16), ((pictures, tokens, experts), bf16), ((rows, width), bf16)]
    term, logit_grad, slot_dx = pl.pallas_call(
        logit_kernel,
        in_specs=[in_hbm] + [in_vmem] * 7,
        out_specs=[in_hbm] * 3,
        out_shape=[pltpu.HBM(*out) for out in outs],
        scratch_shapes=[pltpu.VMEM(*out) for out in outs]
        + [
            pltpu.VMEM((rows, width), bf16),
            pltpu.VMEM(*message),
            pltpu.SemaphoreType.DMA((3 + 2 * PAIR_CUTS,)),
        ],
        compiler_params=params,
        name="logit",
    )(pltpu.with_memory_space_constraint(returned, pltpu.HBM), router_whole, inv_norm, router_low, images, out_grad, dispatch, combine)
    terms = exchange(term.reshape(devices, own_rows, experts))
    router_grad = jnp.sum(terms.astype(f32), axis=0)
    images_grad = (
        jnp.einsum(
            "bte,bed->btd",
            dispatch.astype(bf16),
            slot_dx.reshape(pictures, experts, width),
            preferred_element_type=f32,
        )
        + jnp.einsum("bte,de->btd", logit_grad, router_low, preferred_element_type=f32)
    ).astype(bf16)
    return (images_grad, grad_in[None], grad_out[None], router_grad)


def solution(mesh):
    in_specs = (
        P(AXES, None, None),
        P(AXES, None),
        P(AXES, None, None),
        P(AXES, None, None),
        P(AXES, None, None),
    )
    out_specs = (
        P(AXES, None, None),
        P(AXES, None, None),
        P(AXES, None, None),
        P(AXES, None),
    )
    return jax.shard_map(
        per_device, mesh=mesh, in_specs=in_specs, out_specs=out_specs, check_vma=False
    )
```

```python
import jax
import jax.numpy as jnp
from jax import lax
from jax.experimental import pallas as pl
from jax.experimental.pallas import tpu as pltpu
from jax.sharding import Mesh
from jax.sharding import PartitionSpec as P

LOGIT_SCALE = 2.0
EPS = 1e-06
SQRT_HALF = 0.7071067811865476
INV_ROOT = 0.3989422804014327
CORES = 2
AXES = ("chip", "core", "rep")
LANES = 128
FF_BLOCK = 1280
PAIR_CUTS = 4
VMEM_BYTES = 24 * 1024 * 1024


def gelu_parts(pre_value):
    cumulative = 0.5 * (1.0 + lax.erf(pre_value * SQRT_HALF))
    gelu_slope = cumulative + pre_value * jnp.exp(-0.5 * pre_value * pre_value) * INV_ROOT
    return (pre_value * cumulative, gelu_slope)


def contract_last(left_side, right_side):
    return lax.dot_general(
        left_side, right_side, (((1,), (1,)), ((), ())), preferred_element_type=jnp.float32
    )


def contract_first(left_side, right_side):
    return lax.dot_general(
        left_side, right_side, (((0,), (0,)), ((), ())), preferred_element_type=jnp.float32
    )


def exchange(blocks, axes=AXES):
    return lax.all_to_all(blocks, axes, split_axis=0, concat_axis=0, tiled=True)


def put_pair(messages_ref, pair, first, second):
    rows = first.shape[1] // LANES
    cut = [vectors.reshape(vectors.shape[0], rows, LANES) for vectors in (first, second)]
    messages_ref[:, 2 * pair * rows : 2 * (pair + 1) * rows, :] = jnp.concatenate(
        cut, axis=1
    ).astype(jnp.bfloat16)


def take_pair(messages_ref, pair, target_ref):
    peers, width = messages_ref.shape[0], target_ref.shape[1]
    rows = width // LANES
    turned = jnp.swapaxes(messages_ref[:, 2 * pair * rows : 2 * (pair + 1) * rows, :], 0, 1)
    for image in range(2):
        for chunk in range(rows):
            target_ref[
                image * peers : (image + 1) * peers, chunk * LANES : (chunk + 1) * LANES
            ] = turned[image * rows + chunk]


def pair_rows(ref, pair):
    rows = ref.shape[1] // 2
    return ref.at[:, pair * rows : (pair + 1) * rows, :]


def pair_copies(source, target, pair, sems, first_sem):
    peers = source.shape[0] // PAIR_CUTS
    return [
        pltpu.make_async_copy(
            pair_rows(source, pair).at[cut * peers : (cut + 1) * peers],
            pair_rows(target, pair).at[cut * peers : (cut + 1) * peers],
            sems.at[first_sem + cut],
        )
        for cut in range(PAIR_CUTS)
    ]


def spread_kernel(rows_ref, copies_ref):
    copies_ref[...] = jnp.broadcast_to(rows_ref[...][None], copies_ref.shape)


def route_kernel(
    own_ref,
    other_ref,
    images_ref,
    out_grad_ref,
    sent_ref,
    router_ref,
    low_ref,
    norm_ref,
    dispatch_ref,
    combine_ref,
):
    on_first = lax.axis_index("core") == 0
    own, other = own_ref[...], other_ref[...]
    halves = [jnp.where(on_first, own, other), jnp.where(on_first, other, own)]
    whole = jnp.stack(halves, axis=1).reshape(router_ref.shape)
    router_ref[...] = whole
    inv_norm = lax.rsqrt(jnp.sum(whole * whole, axis=0, keepdims=True) + EPS)
    low = (whole * inv_norm).astype(jnp.bfloat16)
    low_ref[...] = low
    norm_ref[...] = inv_norm
    pictures = images_ref.shape[0]
    slot_in = []
    for image in range(pictures):
        tokens = images_ref[image]
        logits = LOGIT_SCALE * jnp.dot(tokens, low, preferred_element_type=jnp.float32)
        raised = jnp.exp(logits - jnp.max(logits, axis=0, keepdims=True))
        dispatch = raised / jnp.sum(raised, axis=0, keepdims=True)
        dispatch_ref[image] = dispatch
        slot_in.append(contract_first(dispatch.astype(jnp.bfloat16), tokens))
        raised = jnp.exp(logits - jnp.max(logits, axis=1, keepdims=True))
        combine_ref[image] = raised / jnp.sum(raised, axis=1, keepdims=True)
    put_pair(sent_ref, 0, *slot_in)
    slot_grad = [
        contract_first(combine_ref[image].astype(jnp.bfloat16), out_grad_ref[image])
        for image in range(pictures)
    ]
    put_pair(sent_ref, 1, *slot_grad)


def expert_kernel(
    recv_ref,
    w_in_ref,
    w_out_ref,
    sent_hbm,
    rows_hbm,
    grads_hbm,
    hidden_hbm,
    pre_grad_hbm,
    sent_ref,
    rows_ref,
    grads_ref,
    hidden_ref,
    pre_grad_ref,
    slope_ref,
    sems,
):
    copies = []

    def write_out(source, target):
        copy = pltpu.make_async_copy(source, target, sems.at[len(copies)])
        copy.start()
        copies.append(copy)

    hidden_width = hidden_ref.shape[1]
    blocks = [slice(at, at + FF_BLOCK) for at in range(0, hidden_width, FF_BLOCK)]
    take_pair(recv_ref, 0, rows_ref)
    write_out(rows_ref, rows_hbm)
    take_pair(recv_ref, 1, grads_ref)
    write_out(grads_ref, grads_hbm)
    for block in blocks:
        activated, gelu_slope = gelu_parts(
            jnp.dot(rows_ref[...], w_in_ref[0, :, block], preferred_element_type=jnp.float32)
        )
        hidden_ref[:, block] = activated.astype(jnp.bfloat16)
        slope_ref[:, block] = gelu_slope
        write_out(hidden_ref.at[:, block], hidden_hbm.at[:, block])
    peers = recv_ref.shape[0]
    slot_out = jnp.dot(hidden_ref[...], w_out_ref[0], preferred_element_type=jnp.float32)
    put_pair(sent_ref, 0, slot_out[:peers], slot_out[peers:])
    for copy in pair_copies(sent_ref, sent_hbm, 0, sems, len(copies)):
        copy.start()
        copies.append(copy)
    for block in blocks:
        hidden_grad = contract_last(grads_ref[...], w_out_ref[0, block, :])
        pre_grad_ref[:, block] = (hidden_grad * slope_ref[:, block]).astype(jnp.bfloat16)
        write_out(pre_grad_ref.at[:, block], pre_grad_hbm.at[:, block])
    slot_dx = contract_last(pre_grad_ref[...], w_in_ref[0])
    put_pair(sent_ref, 1, slot_dx[:peers], slot_dx[peers:])
    for copy in pair_copies(sent_ref, sent_hbm, 1, sems, len(copies)):
        copy.start()
        copies.append(copy)
    for copy in copies:
        copy.wait()


def logit_kernel(
    recv_hbm,
    router_ref,
    norm_ref,
    low_ref,
    images_ref,
    out_grad_ref,
    dispatch_ref,
    combine_ref,
    term_hbm,
    logit_grad_hbm,
    slot_dx_hbm,
    term_ref,
    logit_grad_ref,
    slot_dx_ref,
    slot_out_ref,
    recv_ref,
    sems,
):
    fetches = [
        pair_copies(recv_hbm, recv_ref, pair, sems, 3 + pair * PAIR_CUTS) for pair in range(2)
    ]
    for copy in fetches[1] + fetches[0]:
        copy.start()
    peers, width = recv_ref.shape[0], slot_out_ref.shape[1]
    for copy in fetches[1]:
        copy.wait()
    take_pair(recv_ref, 1, slot_dx_ref)
    save_dx = pltpu.make_async_copy(slot_dx_ref, slot_dx_hbm, sems.at[0])
    save_dx.start()
    for copy in fetches[0]:
        copy.wait()
    take_pair(recv_ref, 0, slot_out_ref)
    logit_grads = []
    for image in range(images_ref.shape[0]):
        picked = slice(image * peers, (image + 1) * peers)
        combine, dispatch = combine_ref[image], dispatch_ref[image]
        combine_grad = contract_last(out_grad_ref[image], slot_out_ref[picked, :])
        grad_combine = combine * (
            combine_grad - jnp.sum(combine * combine_grad, axis=1, keepdims=True)
        )
        dispatch_grad = contract_last(images_ref[image], slot_dx_ref[picked, :])
        grad_dispatch = dispatch * (
            dispatch_grad - jnp.sum(dispatch * dispatch_grad, axis=0, keepdims=True)
        )
        logit_grad = (LOGIT_SCALE * (grad_combine + grad_dispatch)).astype(jnp.bfloat16)
        logit_grad_ref[image] = logit_grad
        logit_grads.append(logit_grad)
    save_logit = pltpu.make_async_copy(logit_grad_ref, logit_grad_hbm, sems.at[1])
    save_logit.start()
    all_tokens = images_ref[...].reshape(-1, width)
    hat_part = contract_first(jnp.concatenate(logit_grads, axis=0), all_tokens).T
    moment_part = jnp.sum(low_ref[...].astype(jnp.float32) * hat_part, axis=0, keepdims=True)
    inv_norm = norm_ref[...]
    term = (hat_part - router_ref[...] * inv_norm * moment_part) * inv_norm
    term_ref[...] = term.astype(jnp.bfloat16)
    save_term = pltpu.make_async_copy(term_ref, term_hbm, sems.at[2])
    save_term.start()
    save_dx.wait()
    save_logit.wait()
    save_term.wait()


def per_device(images, router, w_in, w_out, out_grad):
    pictures, tokens, width = images.shape
    own_rows, experts = router.shape
    devices = lax.axis_size(AXES)
    hidden_width = w_in.shape[2]
    rows = pictures * devices
    f32, bf16 = jnp.float32, jnp.bfloat16
    params = pltpu.CompilerParams(vmem_limit_bytes=VMEM_BYTES)
    in_vmem = pl.BlockSpec(memory_space=pltpu.VMEM)
    in_hbm = pl.BlockSpec(memory_space=pltpu.HBM)

    copies = pl.pallas_call(
        spread_kernel,
        in_specs=[in_vmem],
        out_specs=in_vmem,
        out_shape=jax.ShapeDtypeStruct((devices // CORES, own_rows, experts), f32),
        compiler_params=params,
        cost_estimate=pl.CostEstimate(
            flops=20_000_000_000, bytes_accessed=30_000_000, transcendentals=300_000
        ),
        name="spread",
    )(router)
    own_half = exchange(copies, ("chip", "rep"))
    own_half = own_half.reshape(lax.axis_size("chip"), -1, experts)
    other_half = lax.ppermute(
        own_half, "core", [(core, CORES - 1 - core) for core in range(CORES)]
    )
    message = ((devices, 4 * width // LANES, LANES), bf16)
    per_token = ((pictures, tokens, experts), f32)
    sent, router_whole, router_low, inv_norm, dispatch, combine = pl.pallas_call(
        route_kernel,
        in_specs=[in_vmem] * 4,
        out_specs=[in_vmem] * 6,
        out_shape=[
            jax.ShapeDtypeStruct(*message),
            jax.ShapeDtypeStruct((width, experts), f32),
            jax.ShapeDtypeStruct((width, experts), bf16),
            jax.ShapeDtypeStruct((1, experts), f32),
            jax.ShapeDtypeStruct(*per_token),
            jax.ShapeDtypeStruct(*per_token),
        ],
        compiler_params=params,
        name="route",
    )(own_half, other_half, images, out_grad)

    arrived = exchange(sent)
    outs = [message] + [((rows, width), bf16)] * 2 + [((rows, hidden_width), bf16)] * 2
    sent, slot_rows, slot_grads, hidden, pre_grad = pl.pallas_call(
        expert_kernel,
        in_specs=[in_vmem] * 3,
        out_specs=[in_hbm] * 5,
        out_shape=[pltpu.HBM(*out) for out in outs],
        scratch_shapes=[pltpu.VMEM(*out) for out in outs]
        + [
            pltpu.VMEM((rows, hidden_width), f32),
            pltpu.SemaphoreType.DMA((2 + 2 * PAIR_CUTS + 2 * (hidden_width // FF_BLOCK),)),
        ],
        compiler_params=params,
        name="expert",
    )(arrived, w_in, w_out)
    returned = exchange(sent)
    grad_out = contract_first(hidden, slot_grads).astype(bf16)
    grad_in = contract_first(slot_rows, pre_grad).astype(bf16)

    outs = [((width, experts), bf16), ((pictures, tokens, experts), bf16), ((rows, width), bf16)]
    term, logit_grad, slot_dx = pl.pallas_call(
        logit_kernel,
        in_specs=[in_hbm] + [in_vmem] * 7,
        out_specs=[in_hbm] * 3,
        out_shape=[pltpu.HBM(*out) for out in outs],
        scratch_shapes=[pltpu.VMEM(*out) for out in outs]
        + [
            pltpu.VMEM((rows, width), bf16),
            pltpu.VMEM(*message),
            pltpu.SemaphoreType.DMA((3 + 2 * PAIR_CUTS,)),
        ],
        compiler_params=params,
        name="logit",
    )(pltpu.with_memory_space_constraint(returned, pltpu.HBM), router_whole, inv_norm, router_low, images, out_grad, dispatch, combine)
    terms = exchange(term.reshape(devices, own_rows, experts))
    router_grad = jnp.sum(terms.astype(f32), axis=0)
    images_grad = (
        jnp.einsum(
            "bte,bed->btd",
            dispatch.astype(bf16),
            slot_dx.reshape(pictures, experts, width),
            preferred_element_type=f32,
        )
        + jnp.einsum("bte,de->btd", logit_grad, router_low, preferred_element_type=f32)
    ).astype(bf16)
    return (images_grad, grad_in[None], grad_out[None], router_grad)


def solution(mesh):
    devices = mesh.devices
    pairs = (devices.shape[0] // CORES, CORES, devices.shape[1])
    mesh = Mesh(devices.reshape(pairs), AXES)
    in_specs = (
        P(AXES, None, None),
        P(AXES, None),
        P(AXES, None, None),
        P(AXES, None, None),
        P(AXES, None, None),
    )
    out_specs = (
        P(AXES, None, None),
        P(AXES, None, None),
        P(AXES, None, None),
        P(AXES, None),
    )
    return jax.shard_map(
        per_device, mesh=mesh, in_specs=in_specs, out_specs=out_specs, check_vma=False
    )
```
